256 devices in a mesh: dp: 128 (over y_lo, x, z, core), group: 2 (over y_hi).
Axes of the slice: x: 4, y: 4 (y_hi: 2, y_lo: 2; y = y_hi * 2 + y_lo), z: 8, core: 2. Of those that a mesh axis runs over, the one named last changes fastest.
Arguments:
- inputs: bfloat16 [256, 64, 5120], P('dp'), may hold values from -6 to 6
- out_grads: bfloat16 [256, 64, 8192], P('dp'), may hold values from -6 to 6
- proj_in: bfloat16 [5120, 64], replicated, may hold values from -0.078125 to 0.078125
- proj_out: bfloat16 [8192, 64], P(None, 'group'), may hold values from -0.0625 to 0.0625
- store: bfloat16 [131072, 4096], P('dp', 'group'), may hold values from -6 to 6
- valid: bfloat16 [2048, 4096], P('dp', 'group'), may hold values from -6 to 6
- owner: int32 [256], replicated, may hold values from 0 to 255, each once
Outputs:
- scores: bfloat16 [131072, 2048], P('dp', 'group')
The draws below stay inside these ranges and needn't reach their ends.
Inputs may be any that keep to these rules, and one draw needn't show every extreme that they name: owner is a permutation of the 256 fresh slots.
All inputs are finite; a program needn't handle non-finite values.
Results may differ from the reference program's by a relative error of at most 0.0024.
Values may be sent and summed in bfloat16 or wider, within the bound.
No kernel may reach another device: no remote copies, remote signals or barrier semaphores. Data moves between devices by JAX's collectives and lax.ppermute only.
A program may use at most 128 MiB of HBM per device.

```python
import jax
import jax.numpy as jnp
from jax import lax

D_IN = 5120
D_OUT = 8192
K_IN = 64
K_OUT = 64
SKETCH = 4096
EX_DEV = 2
SEQ = 64
STORE_DEV = 1024
NEW = 256
STORE = 131072
VAL = 2048
N_DP = 128


def shard_levels(key, extent, cuts, smallest, high):
    factor_of, own = 1.0, jax.random.fold_in(key, 6)
    for position, shards_of in cuts:
        steps = jnp.exp(jax.random.uniform(jax.random.fold_in(own, position), (shards_of,), jnp.float32, smallest / len(cuts), high / len(cuts)))
        factor_of = factor_of * jnp.repeat(steps, extent[position] // shards_of).reshape([-1 if axis == position else 1 for axis in range(len(extent))])
    return factor_of


def centred(key, extent, width, reach, cuts=(), held_as=jnp.bfloat16):
    array = width * jax.random.normal(key, extent, jnp.float32)
    if cuts:
        array = array * shard_levels(key, extent, cuts, -0.22, 0.18)
    return jnp.clip(array, -reach, reach).astype(held_as)


def setup_inputs(seed: int = 0) -> dict:
    keys = jax.random.split(jax.random.key(seed), 8)
    inputs = centred(keys[0], (NEW, SEQ, D_IN), 1.0, 6.0, ((0, 128),))
    out_grads = centred(keys[1], (NEW, SEQ, D_OUT), 1.0, 6.0, ((0, 128),))
    proj_in = centred(keys[2], (D_IN, K_IN), D_IN ** -0.5, 0.078125)
    proj_out = centred(keys[3], (D_OUT, K_OUT), D_OUT ** -0.5, 0.0625, ((1, 2),))
    store = centred(keys[4], (STORE, SKETCH), 1.0, 6.0, ((0, 128), (1, 2)))
    valid = centred(keys[5], (VAL, SKETCH), 1.0, 6.0, ((0, 128), (1, 2)))
    owner = jax.random.permutation(keys[6], NEW).astype(jnp.int32)
    return dict(inputs=inputs, out_grads=out_grads, proj_in=proj_in, proj_out=proj_out, store=store, valid=valid, owner=owner)


def reference(inputs, out_grads, proj_in, proj_out, store, valid, owner):
    lin = jnp.dot(inputs.reshape(NEW * SEQ, D_IN), proj_in, preferred_element_type=jnp.float32).astype(jnp.bfloat16)
    lout = jnp.dot(out_grads.reshape(NEW * SEQ, D_OUT), proj_out, preferred_element_type=jnp.float32).astype(jnp.bfloat16)
    lin = lin.reshape(NEW, SEQ, K_IN).astype(jnp.float32)
    lout = lout.reshape(NEW, SEQ, K_OUT).astype(jnp.float32)
    sketch = jnp.einsum("nso,nsi->noi", lout, lin) * (SEQ ** -0.5)
    sketch = sketch.reshape(NEW, SKETCH).astype(jnp.bfloat16)
    slot_rows = (owner // EX_DEV) * STORE_DEV + owner % EX_DEV
    updated = store.at[slot_rows.astype(jnp.int32)].set(sketch)
    blocks = updated.reshape(N_DP, STORE_DEV, SKETCH)

    def score_block(block):
        total = lax.dot_general(block, valid, (((1,), (1,)), ((), ())), preferred_element_type=jnp.float32)
        return (total * (SKETCH ** -0.5)).astype(jnp.bfloat16)

    return lax.map(score_block, blocks).reshape(STORE, VAL)
```

```python
import jax
import jax.numpy as jnp
from jax import lax
from jax.sharding import Mesh, PartitionSpec as P

DP = ("yl", "x", "z", "c")
SIZES = {"yl": 2, "x": 4, "z": 8, "c": 2, "yh": 2}


def shifted(array, axis, by):
    size = SIZES[axis]
    return lax.ppermute(array, axis, [(i, (i + by) % size) for i in range(size)])


def dot_t(left, right):
    return lax.dot_general(
        left, right, (((1,), (1,)), ((), ())), preferred_element_type=jnp.float32
    )


def make_sketch(inputs, out_grads, proj_in, proj_out):
    examples, length, width_in = inputs.shape
    width_out = out_grads.shape[2]
    lin = jnp.dot(
        inputs.reshape(examples * length, width_in), proj_in, preferred_element_type=jnp.float32
    ).astype(jnp.bfloat16)
    lout = jnp.dot(
        out_grads.reshape(examples * length, width_out),
        proj_out,
        preferred_element_type=jnp.float32,
    ).astype(jnp.bfloat16)
    lin = lin.reshape(examples, length, -1)
    lout = lout.reshape(examples, length, -1)
    sketch = jnp.einsum("nso,nsi->noi", lout, lin, preferred_element_type=jnp.float32) * length ** (
        -0.5
    )
    return sketch.reshape(examples, -1).astype(jnp.bfloat16)


def local(inputs, out_grads, proj_in, proj_out, store, valid, owner):
    yl, x, z, c, yh = (lax.axis_index(a) for a in ("yl", "x", "z", "c", "yh"))
    nx, nz, nc = SIZES["x"], SIZES["z"], SIZES["c"]
    examples = inputs.shape[0]
    rows_v = valid.shape[0]

    received = shifted(store, "yh", 1)

    sketch = make_sketch(inputs, out_grads, proj_in, proj_out)
    half = sketch.shape[1]

    first = jnp.concatenate([valid, sketch], axis=0)
    first = jnp.concatenate([first, shifted(first, "yh", 1)], axis=1)
    other = shifted(first, "yl", 1)
    mine_v = jnp.where(yl == yh, first[:rows_v], other[:rows_v])
    second = jnp.concatenate([mine_v, first[rows_v:], other[rows_v:]], axis=0)

    pieces = [second] + [shifted(second, "x", k) for k in range(1, nx)]
    block = jnp.zeros((nx, rows_v, 2 * half), valid.dtype)
    for k, piece in enumerate(pieces):
        block = lax.dynamic_update_slice(block, piece[None, :rows_v], ((x - k) % nx, 0, 0))
    block = block.reshape(nx * rows_v, 2 * half)
    known = jnp.concatenate([piece[rows_v:] for piece in pieces], axis=0)

    def dp_index(yl_, x_, z_, c_):
        return ((yl_ * nx + x_) * nz + z_) * nc + c_

    from_x = (x - jnp.arange(nx, dtype=jnp.int32)) % nx
    from_yl = (yl + jnp.arange(2, dtype=jnp.int32)) % 2
    example = dp_index(from_yl[None, :, None], from_x[:, None, None], z, c) * examples
    example = (example + jnp.arange(examples, dtype=jnp.int32)).reshape(-1)
    slot_of = owner[example]
    to = dp_index(yl, x, jnp.arange(nz, dtype=jnp.int32)[:, None], jnp.arange(nc, dtype=jnp.int32))
    slot = (to[:, :, None] * examples + jnp.arange(examples, dtype=jnp.int32)).reshape(-1)
    picker = (slot[:, None] == slot_of[None, :]).astype(jnp.bfloat16)
    shares = jnp.dot(picker, known, preferred_element_type=jnp.float32).astype(jnp.bfloat16)
    shares = shares.reshape(nz, nc * examples, 2 * half)

    def share(offset):
        return lax.dynamic_index_in_dim(shares, (z + offset) % nz, 0, keepdims=False)

    rows_b = block.shape[0]
    cut = rows_b // 2
    full = jnp.zeros((nz, rows_b, 2 * half), valid.dtype)
    full = lax.dynamic_update_slice(full, block[None], (z, 0, 0))
    ahead, back = block, block
    ahead_s, back_s = share(4), share(-3)
    for k in range(1, 4):
        ahead_all = shifted(jnp.concatenate([ahead, ahead_s], axis=0), "z", 1)
        back_all = shifted(jnp.concatenate([back, back_s], axis=0), "z", -1)
        ahead, ahead_s = ahead_all[:rows_b], ahead_all[rows_b:] + share(4 - k)
        back, back_s = back_all[:rows_b], back_all[rows_b:] + share(k - 3)
        full = lax.dynamic_update_slice(full, ahead[None], ((z - k) % nz, 0, 0))
        full = lax.dynamic_update_slice(full, back[None], ((z + k) % nz, 0, 0))
    ahead_all = shifted(jnp.concatenate([ahead[:cut], ahead_s], axis=0), "z", 1)
    back_half = shifted(back[cut:], "z", -1)
    far = jnp.concatenate([ahead_all[:cut], back_half], axis=0)
    full = lax.dynamic_update_slice(full, far[None], ((z - 4) % nz, 0, 0))
    fresh = (ahead_all[cut:] + back_s).reshape(nc, examples, 2 * half)

    swap = jnp.concatenate(
        [
            full.reshape(nz * rows_b, 2 * half),
            lax.dynamic_index_in_dim(fresh, 1 - c, 0, keepdims=False),
        ],
        axis=0,
    )
    swapped = shifted(swap, "c", 1)
    fresh = lax.dynamic_index_in_dim(fresh, c, 0, keepdims=False) + swapped[nz * rows_b :]
    twin = swapped[: nz * rows_b].reshape(nz, nx, 1, rows_v, 2 * half)
    full = full.reshape(nz, nx, 1, rows_v, 2 * half)
    both = jnp.where(
        c == 0, jnp.concatenate([full, twin], axis=2), jnp.concatenate([twin, full], axis=2)
    )
    whole = both.transpose(1, 0, 2, 3, 4).reshape(nx * nz * nc * rows_v, 2 * half)

    factor = (2 * half) ** (-0.5)
    total = dot_t(store, whole[:, :half])
    total = lax.dynamic_update_slice(total, dot_t(fresh, whole), (0, 0))
    rest = dot_t(received, whole[:, half:])
    row = lax.broadcasted_iota(jnp.int32, total.shape, 0)
    return ((total + jnp.where(row < examples, 0.0, rest)) * factor).astype(jnp.bfloat16)


def solution(mesh):
    fine = Mesh(mesh.devices.reshape(2, 4, 8, 2, 2), ("yl", "x", "z", "c", "yh"))
    return jax.shard_map(
        local,
        mesh=fine,
        in_specs=(
            P(DP, None, None),
            P(DP, None, None),
            P(),
            P(None, "yh"),
            P(DP, "yh"),
            P(DP, "yh"),
            P(),
        ),
        out_specs=P(DP, "yh"),
        check_vma=False,
    )
```

```python
import functools

import jax
import jax.numpy as jnp
from jax import lax
from jax.experimental import pallas as pl
from jax.experimental.pallas import tpu as pltpu
from jax.sharding import Mesh, PartitionSpec as P

DP = ("yl", "x", "z", "c")
SIZES = {"yl": 2, "x": 4, "z": 8, "c": 2, "yh": 2}
SCALE_ROWS = 16
BLOCK = 256
TINY = 1e-37


def shifted(array, axis, by):
    size = SIZES[axis]
    return lax.ppermute(array, axis, [(i, (i + by) % size) for i in range(size)])


def paired(array, axis, bit):
    size = SIZES[axis]
    return lax.ppermute(array, axis, [(i, i ^ bit) for i in range(size)])


def dot_t(left, right):
    return lax.dot_general(
        left, right, (((1,), (1,)), ((), ())), preferred_element_type=jnp.float32
    )


def make_sketch(inputs, out_grads, proj_in, proj_out):
    examples, length, width_in = inputs.shape
    width_out = out_grads.shape[2]
    lin = jnp.dot(
        inputs.reshape(examples * length, width_in), proj_in, preferred_element_type=jnp.float32
    ).astype(jnp.bfloat16)
    lout = jnp.dot(
        out_grads.reshape(examples * length, width_out),
        proj_out,
        preferred_element_type=jnp.float32,
    ).astype(jnp.bfloat16)
    lin = lin.reshape(examples, length, -1)
    lout = lout.reshape(examples, length, -1)
    sketch = jnp.einsum("nso,nsi->noi", lout, lin, preferred_element_type=jnp.float32) * length ** (
        -0.5
    )
    return sketch.reshape(examples, -1).astype(jnp.bfloat16)


def partial_kernel(own_ref, twin_ref, store_ref, out_ref):
    n = own_ref.shape[0]
    store = store_ref[...]
    a = dot_t(own_ref[...], store)
    b = dot_t(twin_ref[...], store)
    top = jnp.maximum(
        jnp.max(jnp.abs(a), axis=0, keepdims=True), jnp.max(jnp.abs(b), axis=0, keepdims=True)
    )
    power = jnp.ceil(jnp.log2(jnp.maximum(top, TINY)))
    scale = jnp.exp2(-power)
    out_ref[:n] = a * scale
    out_ref[n : 2 * n] = b * scale
    out_ref[2 * n :] = jnp.broadcast_to(power, (SCALE_ROWS, power.shape[1]))


def partial_scores(own, twin, store):
    n, width = own.shape
    rows = store.shape[0]
    return pl.pallas_call(
        partial_kernel,
        grid=(rows // BLOCK,),
        in_specs=[
            pl.BlockSpec((n, width), lambda i: (0, 0)),
            pl.BlockSpec((n, width), lambda i: (0, 0)),
            pl.BlockSpec((BLOCK, width), lambda i: (i, 0)),
        ],
        out_specs=pl.BlockSpec((2 * n + SCALE_ROWS, BLOCK), lambda i: (0, i)),
        out_shape=jax.ShapeDtypeStruct((2 * n + SCALE_ROWS, rows), jnp.float32),
        compiler_params=pltpu.CompilerParams(vmem_limit_bytes=32 * 1024 * 1024),
        cost_estimate=pl.CostEstimate(
            flops=4 * n * width * rows, bytes_accessed=8 * rows * width, transcendentals=0
        ),
    )(own, twin, store)


def own_kernel(store_ref, valid_ref, out_ref):
    out_ref[...] = dot_t(store_ref[...], valid_ref[...])


def own_scores(store, valid):
    rows, width = store.shape
    columns = valid.shape[0]
    return pl.pallas_call(
        own_kernel,
        grid=(rows // BLOCK,),
        in_specs=[
            pl.BlockSpec((BLOCK, width), lambda i: (i, 0)),
            pl.BlockSpec((columns, width), lambda i: (0, 0)),
        ],
        out_specs=pl.BlockSpec((BLOCK, columns), lambda i: (i, 0)),
        out_shape=jax.ShapeDtypeStruct((rows, columns), jnp.float32),
        compiler_params=pltpu.CompilerParams(vmem_limit_bytes=32 * 1024 * 1024),
        cost_estimate=pl.CostEstimate(
            flops=2 * rows * width * columns,
            bytes_accessed=2 * (rows + columns) * width + 4 * rows * columns,
            transcendentals=0,
        ),
    )(store, valid)


def finish_kernel(factor, examples, own_ref, received_ref, fresh_ref, out_ref):
    out_ref[...] = ((own_ref[...] + received_ref[...].T) * factor).astype(out_ref.dtype)

    @pl.when(pl.program_id(0) == 0)
    def _():
        n = fresh_ref.shape[0]
        row = lax.broadcasted_iota(jnp.int32, fresh_ref.shape, 0)
        kept = own_ref[:n] + received_ref[:, :128].T[:n]
        value = jnp.where(row < examples, fresh_ref[...], kept)
        out_ref[:n] = (value * factor).astype(out_ref.dtype)


def finish(own, received, fresh, factor, examples):
    rows, columns = own.shape
    return pl.pallas_call(
        functools.partial(finish_kernel, factor, examples),
        grid=(rows // BLOCK,),
        in_specs=[
            pl.BlockSpec((BLOCK, columns), lambda i: (i, 0)),
            pl.BlockSpec((columns, BLOCK), lambda i: (0, i)),
            pl.BlockSpec(fresh.shape, lambda i: (0, 0)),
        ],
        out_specs=pl.BlockSpec((BLOCK, columns), lambda i: (i, 0)),
        out_shape=jax.ShapeDtypeStruct((rows, columns), jnp.bfloat16),
        compiler_params=pltpu.CompilerParams(vmem_limit_bytes=32 * 1024 * 1024),
        cost_estimate=pl.CostEstimate(
            flops=rows * columns, bytes_accessed=10 * rows * columns, transcendentals=0
        ),
    )(own, received, fresh)


def local(inputs, out_grads, proj_in, proj_out, store, valid, owner):
    yl, x, z, c, yh = (lax.axis_index(a) for a in ("yl", "x", "z", "c", "yh"))
    nx, nz, nc = SIZES["x"], SIZES["z"], SIZES["c"]
    examples = inputs.shape[0]
    rows_v, half = valid.shape
    rows_b = nx * rows_v

    valid_other = shifted(valid, "yl", 1)
    v_out = jnp.where(yl == yh, valid_other, valid)
    v_own = jnp.where(yl == yh, valid, valid_other)

    known = make_sketch(inputs, out_grads, proj_in, proj_out)
    known = jnp.concatenate([known, paired(known, "yl", 1)], axis=0)
    known = jnp.concatenate([known, paired(known, "x", 1)], axis=0)
    known = jnp.concatenate([known, paired(known, "x", 2)], axis=0)

    first = jnp.stack([v_out, v_own])
    pieces = [first] + [shifted(first, "x", k) for k in range(1, nx)]
    block = jnp.zeros((2, nx, rows_v, half), valid.dtype)
    for k, piece in enumerate(pieces):
        block = lax.dynamic_update_slice(block, piece[:, None], (0, (x - k) % nx, 0, 0))
    a0, b0 = block[0].reshape(rows_b, half), block[1].reshape(rows_b, half)

    def dp_index(yl_, x_, z_, c_):
        return ((yl_ * nx + x_) * nz + z_) * nc + c_

    each = jnp.arange(examples, dtype=jnp.int32)
    from_x = x ^ jnp.arange(nx, dtype=jnp.int32)
    from_yl = yl ^ jnp.arange(2, dtype=jnp.int32)
    example = dp_index(from_yl[None, :, None], from_x[:, None, None], z, c) * examples + each
    slot_of = owner[example.reshape(-1)]
    to = dp_index(yl, x, jnp.arange(nz, dtype=jnp.int32)[:, None], jnp.arange(nc, dtype=jnp.int32))
    slot = (to[:, :, None] * examples + each).reshape(-1)
    picker = (slot[:, None] == slot_of[None, :]).astype(jnp.bfloat16)
    shares = jnp.dot(picker, known, preferred_element_type=jnp.float32).astype(jnp.bfloat16)
    shares = shares.reshape(nz, nc * examples, half)

    def share(offset):
        return lax.dynamic_index_in_dim(shares, (z + offset) % nz, 0, keepdims=False)

    full = {
        "out": jnp.zeros((nx, nz, nc, rows_v, half), valid.dtype),
        "own": jnp.zeros((nx, nz, nc, rows_v, half), valid.dtype),
    }

    def fill(name, piece, z_from, c_from):
        full[name] = lax.dynamic_update_slice(
            full[name], piece.reshape(nx, 1, 1, rows_v, half), (0, z_from % nz, c_from, 0, 0)
        )

    received = [jnp.zeros((nx, nz, nc, rows_v, store.shape[0]), jnp.float32)]

    def swap(outs, owns, extra=None):
        blocks = [b for b, _ in outs] + [b for b, _ in owns]
        sent = blocks if extra is None else blocks + [extra]
        got = shifted(jnp.concatenate(sent, axis=0), "c", 1)
        for name, items, base in (("out", outs, 0), ("own", owns, len(outs))):
            for j, (b, z_from) in enumerate(items):
                fill(name, b, z_from, c)
                at = (base + j) * rows_b
                fill(name, got[at : at + rows_b], z_from, 1 - c)
        if outs:
            mine = jnp.concatenate([b for b, _ in outs], axis=0)
            n = mine.shape[0]
            part = partial_scores(mine, got[:n], store).astype(jnp.float16)
            part = shifted(part, "yh", 1).astype(jnp.float32)
            part = part[: 2 * n] * jnp.exp2(part[2 * n : 2 * n + 1])
            for side, c_from in ((0, c), (1, 1 - c)):
                for j, (_, z_from) in enumerate(outs):
                    at = side * n + j * rows_b
                    piece = part[at : at + rows_b].reshape(nx, 1, 1, rows_v, -1)
                    received[0] = lax.dynamic_update_slice(
                        received[0], piece, (0, z_from % nz, c_from, 0, 0)
                    )
        return got[len(blocks) * rows_b :]

    def both_ways(ahead, back):
        return (
            shifted(jnp.concatenate(ahead, axis=0), "z", 1),
            shifted(jnp.concatenate(back, axis=0), "z", -1),
        )

    cut = rows_b // 2
    swap([(a0, z)], [])
    up, down = both_ways([a0], [a0])
    a_up, a_down = up, down
    swap([(a_up, z - 1), (a_down, z + 1)], [(b0, z)])

    up, down = both_ways([a_up, b0, share(4)], [a_down, b0, share(-3)])
    a_up, b_up, s_up = up[:rows_b], up[rows_b : 2 * rows_b], up[2 * rows_b :] + share(3)
    a_down, b_down, s_down = (
        down[:rows_b],
        down[rows_b : 2 * rows_b],
        down[2 * rows_b :] + share(-2),
    )
    swap([(a_up, z - 2), (a_down, z + 2)], [(b_up, z - 1), (b_down, z + 1)])

    up, down = both_ways([a_up, b_up, s_up], [a_down, b_down, s_down])
    a_up, b_up, s_up = up[:rows_b], up[rows_b : 2 * rows_b], up[2 * rows_b :] + share(2)
    a_down, b_down, s_down = (
        down[:rows_b],
        down[rows_b : 2 * rows_b],
        down[2 * rows_b :] + share(-1),
    )
    swap([(a_up, z - 3), (a_down, z + 3)], [(b_up, z - 2), (b_down, z + 2)])

    up, down = both_ways([a_up[:cut], b_up, s_up], [a_down[cut:], b_down, s_down])
    a_far = jnp.concatenate([up[:cut], down[:cut]], axis=0)
    b_up, s_up = up[cut : cut + rows_b], up[cut + rows_b :] + share(1)
    b_down, s_down = down[cut : cut + rows_b], down[cut + rows_b :] + share(0)
    swap([(a_far, z - 4)], [(b_up, z - 3), (b_down, z + 3)])

    up, down = both_ways([b_up[:cut], s_up], [b_down[cut:]])
    b_far = jnp.concatenate([up[:cut], down], axis=0)
    fresh = (up[cut:] + s_down).reshape(nc, examples, half)
    got = swap([], [(b_far, z - 4)], lax.dynamic_index_in_dim(fresh, 1 - c, 0, keepdims=False))
    fresh = lax.dynamic_index_in_dim(fresh, c, 0, keepdims=False) + got

    fresh = jnp.pad(fresh, ((0, 16 - examples), (0, 0)))
    whole_out = full["out"].reshape(nx * nz * nc * rows_v, half)
    whole_own = full["own"].reshape(nx * nz * nc * rows_v, half)
    fresh_scores = dot_t(fresh, whole_own) + shifted(dot_t(fresh, whole_out), "yh", 1)

    own = own_scores(store, whole_own)
    partner = received[0].reshape(nx * nz * nc * rows_v, store.shape[0])
    return finish(own, partner, fresh_scores, (2 * half) ** (-0.5), examples)


def solution(mesh):
    fine = Mesh(mesh.devices.reshape(2, 4, 8, 2, 2), ("yl", "x", "z", "c", "yh"))
    return jax.shard_map(
        local,
        mesh=fine,
        in_specs=(
            P(DP, None, None),
            P(DP, None, None),
            P(),
            P(None, "yh"),
            P(DP, "yh"),
            P(DP, "yh"),
            P(),
        ),
        out_specs=P(DP, "yh"),
        check_vma=False,
    )
```

```python
import functools

import jax
import jax.numpy as jnp
from jax import lax
from jax.experimental import pallas as pl
from jax.experimental.pallas import tpu as pltpu
from jax.sharding import Mesh, PartitionSpec as P

DP = ("yl", "x", "z", "c")
SIZES = {"yl": 2, "x": 4, "z": 8, "c": 2, "yh": 2}
MIB = 1024 * 1024
BLOCK = 256
FILL_FLOPS = 20_000_000_000


def shifted(array, axis, by):
    size = SIZES[axis]
    return lax.ppermute(array, axis, [(i, (i + by) % size) for i in range(size)])


def paired(array, axis, bit):
    size = SIZES[axis]
    return lax.ppermute(array, axis, [(i, i ^ bit) for i in range(size)])


def dot_t(left, right):
    return lax.dot_general(
        left, right, (((1,), (1,)), ((), ())), preferred_element_type=jnp.float32
    )


def make_sketch(inputs, out_grads, proj_in, proj_out):
    examples, length, width_in = inputs.shape
    width_out = out_grads.shape[2]
    lin = jnp.dot(
        inputs.reshape(examples * length, width_in), proj_in, preferred_element_type=jnp.float32
    ).astype(jnp.bfloat16)
    lout = jnp.dot(
        out_grads.reshape(examples * length, width_out),
        proj_out,
        preferred_element_type=jnp.float32,
    ).astype(jnp.bfloat16)
    lin = lin.reshape(examples, length, -1)
    lout = lout.reshape(examples, length, -1)
    sketch = jnp.einsum("nso,nsi->noi", lout, lin, preferred_element_type=jnp.float32) * length ** (
        -0.5
    )
    return sketch.reshape(examples, -1).astype(jnp.bfloat16)


def own_kernel(store_ref, valid_ref, fresh_ref, out_ref, fresh_out_ref):
    out_ref[...] = dot_t(valid_ref[...], store_ref[...])

    @pl.when(pl.program_id(0) == 0)
    def _():
        fresh_out_ref[...] = dot_t(fresh_ref[...], valid_ref[...])


def own_scores(store, valid, fresh):
    rows, half = store.shape
    columns = valid.shape[0]
    return pl.pallas_call(
        own_kernel,
        grid=(rows // BLOCK,),
        in_specs=[
            pl.BlockSpec((BLOCK, half), lambda i: (i, 0)),
            pl.BlockSpec((columns, half), lambda i: (0, 0), pipeline_mode=pl.Buffered(1)),
            pl.BlockSpec(fresh.shape, lambda i: (0, 0)),
        ],
        out_specs=[
            pl.BlockSpec((columns, BLOCK), lambda i: (0, i)),
            pl.BlockSpec((fresh.shape[0], columns), lambda i: (0, 0)),
        ],
        out_shape=[
            jax.ShapeDtypeStruct((columns, rows), jnp.float32),
            jax.ShapeDtypeStruct((fresh.shape[0], columns), jnp.float32),
        ],
        compiler_params=pltpu.CompilerParams(vmem_limit_bytes=20 * MIB),
        cost_estimate=pl.CostEstimate(flops=0, bytes_accessed=0, transcendentals=0),
    )(store, valid, fresh)


def last_kernel(factor, examples, other_ref, valid_ref, own_ref, fresh_other, fresh_own, out_ref):
    total = own_ref[...] + dot_t(valid_ref[...], other_ref[...])
    out_ref[...] = (total.T * factor).astype(out_ref.dtype)

    @pl.when(pl.program_id(0) == 0)
    def _():
        n = fresh_own.shape[0]
        value = fresh_own[...] + dot_t(fresh_other[...], valid_ref[...])
        value = (value * factor).astype(out_ref.dtype)
        row = lax.broadcasted_iota(jnp.int32, value.shape, 0)
        out_ref[:n] = jnp.where(row < examples, value, out_ref[:n])


def last_scores(other, valid, own, fresh_other, fresh_own, factor, examples):
    rows, half = other.shape
    columns = valid.shape[0]
    return pl.pallas_call(
        functools.partial(last_kernel, factor, examples),
        grid=(rows // BLOCK,),
        in_specs=[
            pl.BlockSpec((BLOCK, half), lambda i: (i, 0)),
            pl.BlockSpec((columns, half), lambda i: (0, 1), pipeline_mode=pl.Buffered(1)),
            pl.BlockSpec((columns, BLOCK), lambda i: (0, i)),
            pl.BlockSpec(fresh_other.shape, lambda i: (0, 0)),
            pl.BlockSpec(fresh_own.shape, lambda i: (0, 0)),
        ],
        out_specs=pl.BlockSpec((BLOCK, columns), lambda i: (i, 0)),
        out_shape=jax.ShapeDtypeStruct((rows, columns), jnp.bfloat16),
        compiler_params=pltpu.CompilerParams(vmem_limit_bytes=24 * MIB),
        cost_estimate=pl.CostEstimate(flops=0, bytes_accessed=0, transcendentals=0),
    )(other, valid, own, fresh_other, fresh_own)


def fill_kernel(table_ref, mine_ref, twin_ref, *refs):
    out_ref = refs[-1]
    n = pl.num_programs(0) // 2

    @pl.when(pl.program_id(0) < n)
    def _():
        out_ref[:, 0, 0] = mine_ref[0]

    @pl.when(pl.program_id(0) >= n)
    def _():
        out_ref[:, 0, 0] = twin_ref[0]


def filled(whole, shape, mine, twin, table):
    nx, _, _, rows_v, width = shape
    n = mine.shape[0] // (nx * rows_v)
    operands = [table, mine.reshape(n, nx, rows_v, width), twin.reshape(n, nx, rows_v, width)]
    specs = [
        pl.BlockSpec((1, nx, rows_v, width), lambda s, t: (jnp.minimum(s, n - 1), 0, 0, 0)),
        pl.BlockSpec((1, nx, rows_v, width), lambda s, t: (jnp.maximum(s - n, 0), 0, 0, 0)),
    ]
    if whole is not None:
        operands.append(whole)
        specs.append(pl.BlockSpec(memory_space=pl.ANY))
    return pl.pallas_call(
        fill_kernel,
        grid_spec=pltpu.PrefetchScalarGridSpec(
            num_scalar_prefetch=1,
            grid=(2 * n,),
            in_specs=specs,
            out_specs=pl.BlockSpec(
                (nx, 1, 1, rows_v, width), lambda s, t: (0, t[2 * s], t[2 * s + 1], 0, 0)
            ),
        ),
        out_shape=jax.ShapeDtypeStruct(shape, mine.dtype),
        input_output_aliases={} if whole is None else {3: 0},
        compiler_params=pltpu.CompilerParams(vmem_limit_bytes=16 * MIB),
        cost_estimate=pl.CostEstimate(
            flops=FILL_FLOPS, bytes_accessed=4 * n * nx * rows_v * width, transcendentals=0
        ),
    )(*operands)


def local(inputs, out_grads, proj_in, proj_out, store, valid, owner):
    yl, x, z, c, yh = (lax.axis_index(a) for a in ("yl", "x", "z", "c", "yh"))
    nx, nz, nc = SIZES["x"], SIZES["z"], SIZES["c"]
    examples = inputs.shape[0]
    rows_v, half = valid.shape
    rows_b = nx * rows_v
    rows_s = nc * examples

    def at(y):
        return (y % 2) * 2 + y // 2

    near = lax.ppermute(valid, ("yl", "yh"), [(at(i), at(j)) for i, j in ((0, 1), (1, 3), (2, 0), (3, 2))])
    cross = lax.ppermute(valid, ("yl", "yh"), [(at(1), at(2)), (at(2), at(1))])
    here = jnp.concatenate(
        [jnp.where(yl == yh, valid, near), jnp.where(yl == yh, near, cross)], axis=1
    )

    known = make_sketch(inputs, out_grads, proj_in, proj_out)
    known = jnp.concatenate([known, paired(known, "yl", 1)], axis=0)

    known, waited = lax.optimization_barrier((known, store))
    other = shifted(waited, "yh", 1)

    known = jnp.concatenate([known, paired(known, "x", 1)], axis=0)
    known, here = lax.optimization_barrier((known, here))

    pieces = [here] + [shifted(here, "x", k) for k in range(1, nx)]
    block = jnp.zeros((nx, rows_v, 2 * half), valid.dtype)
    for k, piece in enumerate(pieces):
        block = lax.dynamic_update_slice(block, piece[None], ((x - k) % nx, 0, 0))
    block = block.reshape(rows_b, 2 * half)

    whole = [None]

    def fill_all(mine, twin, steps):
        froms = [((z + step) % nz, c) for step in steps] + [((z + step) % nz, 1 - c) for step in steps]
        table = jnp.stack([part for pair in froms for part in pair]).astype(jnp.int32)
        shape = (nx, nz, nc, rows_v, 2 * half)
        whole[0] = filled(whole[0], shape, mine, twin, table)

    def both_ways(ahead, back):
        ahead, back = lax.optimization_barrier((ahead, back))
        return lax.optimization_barrier((shifted(ahead, "z", 1), shifted(back, "z", -1)))

    twin = shifted(block, "c", 1)
    up, down = both_ways(block, block)
    fill_all(block, twin, (0,))

    known = jnp.concatenate([known, paired(known, "x", 2)], axis=0)

    def dp_index(yl_, x_, z_, c_):
        return ((yl_ * nx + x_) * nz + z_) * nc + c_

    each = jnp.arange(examples, dtype=jnp.int32)
    from_x = x ^ jnp.arange(nx, dtype=jnp.int32)
    from_yl = yl ^ jnp.arange(2, dtype=jnp.int32)
    example = dp_index(from_yl[None, :, None], from_x[:, None, None], z, c) * examples + each
    slot_of = owner[example.reshape(-1)]
    to_z = (z + jnp.arange(nz, dtype=jnp.int32)) % nz
    to = dp_index(yl, x, to_z[:, None], jnp.arange(nc, dtype=jnp.int32))
    slot = (to[:, :, None] * examples + each).reshape(-1)
    picker = (slot[:, None] == slot_of[None, :]).astype(jnp.bfloat16)
    shares = jnp.dot(picker, known, preferred_element_type=jnp.float32).astype(jnp.bfloat16)
    shares = jnp.pad(shares, ((0, 0), (0, half)))

    def share(offset):
        first = (offset % nz) * rows_s
        return shares[first : first + rows_s]

    for k in (1, 2, 3):
        mine = jnp.concatenate([up[:rows_b], down[:rows_b]], axis=0)
        twin = shifted(mine, "c", 1)
        s_up, s_down = share(4 - k), share(k - 4)
        if k > 1:
            s_up, s_down = s_up + up[rows_b:], s_down + down[rows_b:]
        if k < 3:
            ahead, back = up[:rows_b], down[:rows_b]
        else:
            ahead, back = up[: rows_b // 2], down[rows_b // 2 : rows_b]
        up, down = both_ways(
            jnp.concatenate([ahead, s_up], axis=0), jnp.concatenate([back, s_down], axis=0)
        )
        fill_all(mine, twin, (-k, k))
        if k == 1:
            s_far = shifted(share(4), "z", 4)
    cut = rows_b // 2
    far = jnp.concatenate([up[:cut], down[:cut]], axis=0)
    fresh = (up[cut:] + down[cut:]) + (s_far + share(0))
    fresh = fresh.reshape(nc, examples, 2 * half)
    leave = jnp.where(c == 0, fresh[1], fresh[0])
    got = shifted(jnp.concatenate([far, leave], axis=0), "c", 1)
    fill_all(far, got[:rows_b], (4,))
    fresh = jnp.where(c == 0, fresh[0], fresh[1]) + got[rows_b:]

    fresh = jnp.pad(fresh[:, :half], ((0, 16 - examples), (0, 0)))
    fresh_other = shifted(fresh, "yh", 1)
    valid_all = whole[0].reshape(nx * nz * nc * rows_v, 2 * half)
    own, fresh_own = own_scores(store, valid_all, fresh)
    other, own = lax.optimization_barrier((other, own))
    return last_scores(
        other, valid_all, own, fresh_other, fresh_own, (2 * half) ** (-0.5), examples
    )


def solution(mesh):
    fine = Mesh(mesh.devices.reshape(2, 4, 8, 2, 2), ("yl", "x", "z", "c", "yh"))
    return jax.shard_map(
        local,
        mesh=fine,
        in_specs=(
            P(DP, None, None),
            P(DP, None, None),
            P(),
            P(None, "yh"),
            P(DP, "yh"),
            P(DP, "yh"),
            P(),
        ),
        out_specs=P(DP, "yh"),
        check_vma=False,
    )
```

```python
import functools

import jax
import jax.numpy as jnp
from jax import lax
from jax.experimental import pallas as pl
from jax.experimental.pallas import tpu as pltpu
from jax.sharding import Mesh, PartitionSpec as P

DP = ("yl", "x", "z", "c")
SIZES = {"yl": 2, "x": 4, "z": 8, "c": 2, "yh": 2}
MIB = 1024 * 1024
BLOCK = 256
FILL_FLOPS = 20_000_000_000


def shifted(array, axis, by):
    size = SIZES[axis]
    return lax.ppermute(array, axis, [(i, (i + by) % size) for i in range(size)])


def paired(array, axis, bit):
    size = SIZES[axis]
    return lax.ppermute(array, axis, [(i, i ^ bit) for i in range(size)])


def dot_t(left, right):
    return lax.dot_general(
        left, right, (((1,), (1,)), ((), ())), preferred_element_type=jnp.float32
    )


def make_sketch(inputs, out_grads, proj_in, proj_out):
    examples, length, width_in = inputs.shape
    width_out = out_grads.shape[2]
    lin = jnp.dot(
        inputs.reshape(examples * length, width_in), proj_in, preferred_element_type=jnp.float32
    ).astype(jnp.bfloat16)
    lout = jnp.dot(
        out_grads.reshape(examples * length, width_out),
        proj_out,
        preferred_element_type=jnp.float32,
    ).astype(jnp.bfloat16)
    lin = lin.reshape(examples, length, -1)
    lout = lout.reshape(examples, length, -1)
    sketch = jnp.einsum("nso,nsi->noi", lout, lin, preferred_element_type=jnp.float32) * length ** (
        -0.5
    )
    return sketch.reshape(examples, -1).astype(jnp.bfloat16)


def own_kernel(store_ref, valid_ref, fresh_ref, out_ref, fresh_out_ref):
    out_ref[...] = dot_t(store_ref[...], valid_ref[...])
    fresh_out_ref[...] = dot_t(fresh_ref[...], valid_ref[...])


def own_scores(store, valid, fresh):
    rows, half = store.shape
    columns = valid.shape[0]
    whole = lambda array: pl.BlockSpec(array.shape, lambda i: (0, 0), pipeline_mode=pl.Buffered(1))
    return pl.pallas_call(
        own_kernel,
        grid=(columns // BLOCK,),
        in_specs=[
            whole(store),
            pl.BlockSpec((BLOCK, half), lambda i: (i, 0)),
            whole(fresh),
        ],
        out_specs=[
            pl.BlockSpec((rows, BLOCK), lambda i: (0, i)),
            pl.BlockSpec((fresh.shape[0], BLOCK), lambda i: (0, i)),
        ],
        out_shape=[
            jax.ShapeDtypeStruct((rows, columns), jnp.float32),
            jax.ShapeDtypeStruct((fresh.shape[0], columns), jnp.float32),
        ],
        compiler_params=pltpu.CompilerParams(vmem_limit_bytes=16 * MIB),
        cost_estimate=pl.CostEstimate(flops=0, bytes_accessed=0, transcendentals=0),
    )(store, valid, fresh)


def last_kernel(factor, examples, other_ref, valid_ref, own_ref, fresh_other, fresh_own, out_ref):
    total = own_ref[...] + dot_t(other_ref[...], valid_ref[...])
    out_ref[...] = (total * factor).astype(out_ref.dtype)
    n = fresh_own.shape[0]
    value = fresh_own[...] + dot_t(fresh_other[...], valid_ref[...])
    value = (value * factor).astype(out_ref.dtype)
    row = lax.broadcasted_iota(jnp.int32, value.shape, 0)
    out_ref[:n] = jnp.where(row < examples, value, out_ref[:n])


def last_scores(other, valid, own, fresh_other, fresh_own, factor, examples):
    rows, half = other.shape
    columns = valid.shape[0]
    whole = lambda array: pl.BlockSpec(array.shape, lambda i: (0, 0), pipeline_mode=pl.Buffered(1))
    return pl.pallas_call(
        functools.partial(last_kernel, factor, examples),
        grid=(columns // BLOCK,),
        in_specs=[
            whole(other),
            pl.BlockSpec((BLOCK, half), lambda i: (i, 1)),
            pl.BlockSpec((rows, BLOCK), lambda i: (0, i)),
            whole(fresh_other),
            pl.BlockSpec((fresh_own.shape[0], BLOCK), lambda i: (0, i)),
        ],
        out_specs=pl.BlockSpec((rows, BLOCK), lambda i: (0, i)),
        out_shape=jax.ShapeDtypeStruct((rows, columns), jnp.bfloat16),
        compiler_params=pltpu.CompilerParams(vmem_limit_bytes=16 * MIB),
        cost_estimate=pl.CostEstimate(flops=0, bytes_accessed=0, transcendentals=0),
    )(other, valid, own, fresh_other, fresh_own)


def fill_kernel(table_ref, mine_ref, twin_ref, *refs):
    out_ref = refs[-1]
    n = pl.num_programs(0) // 2

    @pl.when(pl.program_id(0) < n)
    def _():
        out_ref[:, 0, 0] = mine_ref[0]

    @pl.when(pl.program_id(0) >= n)
    def _():
        out_ref[:, 0, 0] = twin_ref[0]


def filled(whole, shape, mine, twin, table):
    nx, _, _, rows_v, width = shape
    n = mine.shape[0] // (nx * rows_v)
    operands = [table, mine.reshape(n, nx, rows_v, width), twin.reshape(n, nx, rows_v, width)]
    specs = [
        pl.BlockSpec((1, nx, rows_v, width), lambda s, t: (jnp.minimum(s, n - 1), 0, 0, 0)),
        pl.BlockSpec((1, nx, rows_v, width), lambda s, t: (jnp.maximum(s - n, 0), 0, 0, 0)),
    ]
    if whole is not None:
        operands.append(whole)
        specs.append(pl.BlockSpec(memory_space=pl.ANY))
    return pl.pallas_call(
        fill_kernel,
        grid_spec=pltpu.PrefetchScalarGridSpec(
            num_scalar_prefetch=1,
            grid=(2 * n,),
            in_specs=specs,
            out_specs=pl.BlockSpec(
                (nx, 1, 1, rows_v, width), lambda s, t: (0, t[2 * s], t[2 * s + 1], 0, 0)
            ),
        ),
        out_shape=jax.ShapeDtypeStruct(shape, mine.dtype),
        input_output_aliases={} if whole is None else {3: 0},
        compiler_params=pltpu.CompilerParams(vmem_limit_bytes=8 * MIB),
        cost_estimate=pl.CostEstimate(
            flops=FILL_FLOPS, bytes_accessed=4 * n * nx * rows_v * width, transcendentals=0
        ),
    )(*operands)


def local(inputs, out_grads, proj_in, proj_out, store, valid, owner):
    yl, x, z, c, yh = (lax.axis_index(a) for a in ("yl", "x", "z", "c", "yh"))
    nx, nz, nc = SIZES["x"], SIZES["z"], SIZES["c"]
    examples = inputs.shape[0]
    rows_v, half = valid.shape
    rows_b = nx * rows_v
    rows_s = nc * examples

    def at(y):
        return (y % 2) * 2 + y // 2

    near = lax.ppermute(valid, ("yl", "yh"), [(at(i), at(j)) for i, j in ((0, 1), (1, 3), (2, 0), (3, 2))])
    cross = lax.ppermute(valid, ("yl", "yh"), [(at(1), at(2)), (at(2), at(1))])
    here = jnp.concatenate(
        [jnp.where(yl == yh, valid, near), jnp.where(yl == yh, near, cross)], axis=1
    )

    known = make_sketch(inputs, out_grads, proj_in, proj_out)
    known = jnp.concatenate([known, paired(known, "yl", 1)], axis=0)

    known, waited = lax.optimization_barrier((known, store))
    other = shifted(waited, "yh", 1)

    known = jnp.concatenate([known, paired(known, "x", 1)], axis=0)
    known, here = lax.optimization_barrier((known, here))

    pieces = [here] + [shifted(here, "x", k) for k in range(1, nx)]
    block = jnp.zeros((nx, rows_v, 2 * half), valid.dtype)
    for k, piece in enumerate(pieces):
        block = lax.dynamic_update_slice(block, piece[None], ((x - k) % nx, 0, 0))
    block = block.reshape(rows_b, 2 * half)

    whole = [None]

    def fill_all(mine, twin, steps):
        froms = [((z + step) % nz, c) for step in steps] + [((z + step) % nz, 1 - c) for step in steps]
        table = jnp.stack([part for pair in froms for part in pair]).astype(jnp.int32)
        shape = (nx, nz, nc, rows_v, 2 * half)
        whole[0] = filled(whole[0], shape, mine, twin, table)

    def both_ways(ahead, back):
        ahead, back = lax.optimization_barrier((ahead, back))
        return lax.optimization_barrier((shifted(ahead, "z", 1), shifted(back, "z", -1)))

    twin = shifted(block, "c", 1)
    up, down = both_ways(block, block)
    fill_all(block, twin, (0,))

    known = jnp.concatenate([known, paired(known, "x", 2)], axis=0)

    def dp_index(yl_, x_, z_, c_):
        return ((yl_ * nx + x_) * nz + z_) * nc + c_

    each = jnp.arange(examples, dtype=jnp.int32)
    from_x = x ^ jnp.arange(nx, dtype=jnp.int32)
    from_yl = yl ^ jnp.arange(2, dtype=jnp.int32)
    example = dp_index(from_yl[None, :, None], from_x[:, None, None], z, c) * examples + each
    number = jnp.arange(owner.shape[0], dtype=jnp.int32)
    slot_of = jnp.sum(jnp.where(example.reshape(-1, 1) == number, owner, 0), axis=1)
    to_z = (z + jnp.arange(nz, dtype=jnp.int32)) % nz
    to = dp_index(yl, x, to_z[:, None], jnp.arange(nc, dtype=jnp.int32))
    slot = (to[:, :, None] * examples + each).reshape(-1)
    picker = (slot[:, None] == slot_of[None, :]).astype(jnp.bfloat16)
    shares = jnp.dot(picker, known, preferred_element_type=jnp.float32).astype(jnp.bfloat16)
    shares = jnp.pad(shares, ((0, 0), (0, half)))

    def share(offset):
        first = (offset % nz) * rows_s
        return shares[first : first + rows_s]

    for k in (1, 2, 3):
        mine = jnp.concatenate([up[:rows_b], down[:rows_b]], axis=0)
        twin = shifted(mine, "c", 1)
        s_up, s_down = share(4 - k), share(k - 4)
        if k > 1:
            s_up, s_down = s_up + up[rows_b:], s_down + down[rows_b:]
        if k < 3:
            ahead, back = up[:rows_b], down[:rows_b]
        else:
            ahead, back = up[: rows_b // 2], down[rows_b // 2 : rows_b]
        up, down = both_ways(
            jnp.concatenate([ahead, s_up], axis=0), jnp.concatenate([back, s_down], axis=0)
        )
        fill_all(mine, twin, (-k, k))
        if k == 1:
            s_far = shifted(share(4), "z", 4)
    cut = rows_b // 2
    far = jnp.concatenate([up[:cut], down[:cut]], axis=0)
    fresh = (up[cut:] + down[cut:]) + (s_far + share(0))
    fresh = fresh.reshape(nc, examples, 2 * half)
    leave = jnp.where(c == 0, fresh[1], fresh[0])
    got = shifted(jnp.concatenate([far, leave], axis=0), "c", 1)
    fill_all(far, got[:rows_b], (4,))
    fresh = jnp.where(c == 0, fresh[0], fresh[1]) + got[rows_b:]

    fresh = jnp.pad(fresh[:, :half], ((0, 16 - examples), (0, 0)))
    fresh_other = shifted(fresh, "yh", 1)
    valid_all = whole[0].reshape(nx * nz * nc * rows_v, 2 * half)
    own, fresh_own = own_scores(store, valid_all, fresh)
    other, own = lax.optimization_barrier((other, own))
    return last_scores(
        other, valid_all, own, fresh_other, fresh_own, (2 * half) ** (-0.5), examples
    )


def solution(mesh):
    fine = Mesh(mesh.devices.reshape(2, 4, 8, 2, 2), ("yl", "x", "z", "c", "yh"))
    return jax.shard_map(
        local,
        mesh=fine,
        in_specs=(
            P(DP, None, None),
            P(DP, None, None),
            P(),
            P(None, "yh"),
            P(DP, "yh"),
            P(DP, "yh"),
            P(),
        ),
        out_specs=P(DP, "yh"),
        check_vma=False,
    )
```

```python
import functools

import jax
import jax.numpy as jnp
from jax import lax
from jax.experimental import pallas as pl
from jax.experimental.pallas import tpu as pltpu
from jax.sharding import Mesh, PartitionSpec as P

DP = ("yl", "x", "z", "c")
SIZES = {"yl": 2, "x": 4, "z": 8, "c": 2, "yh": 2}
MIB = 1024 * 1024
BLOCK = 256
FILL_FLOPS = 20_000_000_000


def shifted(array, axis, by):
    size = SIZES[axis]
    return lax.ppermute(array, axis, [(i, (i + by) % size) for i in range(size)])


def paired(array, axis, bit):
    size = SIZES[axis]
    return lax.ppermute(array, axis, [(i, i ^ bit) for i in range(size)])


def dot_t(left, right):
    return lax.dot_general(
        left, right, (((1,), (1,)), ((), ())), preferred_element_type=jnp.float32
    )


def make_sketch(inputs, out_grads, proj_in, proj_out):
    examples, length, width_in = inputs.shape
    width_out = out_grads.shape[2]
    lin = jnp.dot(
        inputs.reshape(examples * length, width_in), proj_in, preferred_element_type=jnp.float32
    ).astype(jnp.bfloat16)
    lout = jnp.dot(
        out_grads.reshape(examples * length, width_out),
        proj_out,
        preferred_element_type=jnp.float32,
    ).astype(jnp.bfloat16)
    lin = lin.reshape(examples, length, -1)
    lout = lout.reshape(examples, length, -1)
    sketch = jnp.einsum("nso,nsi->noi", lout, lin, preferred_element_type=jnp.float32) * length ** (
        -0.5
    )
    return sketch.reshape(examples, -1).astype(jnp.bfloat16)


def own_kernel(examples, store_ref, valid_ref, fresh_ref, out_ref):
    out_ref[...] = dot_t(store_ref[...], valid_ref[...])
    n = fresh_ref.shape[0]
    value = dot_t(fresh_ref[...], valid_ref[...])
    row = lax.broadcasted_iota(jnp.int32, value.shape, 0)
    out_ref[:n] = jnp.where(row < examples, value, out_ref[:n])


def own_scores(store, valid, fresh, examples):
    rows, half = store.shape
    columns = valid.shape[0]
    whole = lambda array: pl.BlockSpec(array.shape, lambda i: (0, 0), pipeline_mode=pl.Buffered(1))
    return pl.pallas_call(
        functools.partial(own_kernel, examples),
        grid=(columns // BLOCK,),
        in_specs=[
            whole(store),
            pl.BlockSpec((BLOCK, half), lambda i: (i, 0)),
            whole(fresh),
        ],
        out_specs=pl.BlockSpec((rows, BLOCK), lambda i: (0, i)),
        out_shape=jax.ShapeDtypeStruct((rows, columns), jnp.float32),
        compiler_params=pltpu.CompilerParams(vmem_limit_bytes=16 * MIB),
        cost_estimate=pl.CostEstimate(flops=0, bytes_accessed=0, transcendentals=0),
    )(store, valid, fresh)


def last_kernel(factor, other_ref, valid_ref, own_ref, out_ref):
    total = own_ref[...] + dot_t(other_ref[...], valid_ref[...])
    out_ref[...] = (total * factor).astype(out_ref.dtype)


def last_scores(other, valid, own, factor):
    rows, half = other.shape
    columns = valid.shape[0]
    return pl.pallas_call(
        functools.partial(last_kernel, factor),
        grid=(columns // BLOCK,),
        in_specs=[
            pl.BlockSpec((rows, half), lambda i: (0, 0), pipeline_mode=pl.Buffered(1)),
            pl.BlockSpec((BLOCK, half), lambda i: (i, 1)),
            pl.BlockSpec((rows, BLOCK), lambda i: (0, i)),
        ],
        out_specs=pl.BlockSpec((rows, BLOCK), lambda i: (0, i)),
        out_shape=jax.ShapeDtypeStruct((rows, columns), jnp.bfloat16),
        compiler_params=pltpu.CompilerParams(vmem_limit_bytes=16 * MIB),
        cost_estimate=pl.CostEstimate(flops=0, bytes_accessed=0, transcendentals=0),
    )(other, valid, own)


def fill_kernel(table_ref, mine_ref, twin_ref, *refs):
    out_ref = refs[-1]
    n = pl.num_programs(0) // 2

    @pl.when(pl.program_id(0) < n)
    def _():
        out_ref[:, 0, 0] = mine_ref[0]

    @pl.when(pl.program_id(0) >= n)
    def _():
        out_ref[:, 0, 0] = twin_ref[0]


def filled(whole, shape, mine, twin, table):
    nx, _, _, rows_v, width = shape
    n = mine.shape[0] // (nx * rows_v)
    operands = [table, mine.reshape(n, nx, rows_v, width), twin.reshape(n, nx, rows_v, width)]
    specs = [
        pl.BlockSpec((1, nx, rows_v, width), lambda s, t: (jnp.minimum(s, n - 1), 0, 0, 0)),
        pl.BlockSpec((1, nx, rows_v, width), lambda s, t: (jnp.maximum(s - n, 0), 0, 0, 0)),
    ]
    if whole is not None:
        operands.append(whole)
        specs.append(pl.BlockSpec(memory_space=pl.ANY))
    return pl.pallas_call(
        fill_kernel,
        grid_spec=pltpu.PrefetchScalarGridSpec(
            num_scalar_prefetch=1,
            grid=(2 * n,),
            in_specs=specs,
            out_specs=pl.BlockSpec(
                (nx, 1, 1, rows_v, width), lambda s, t: (0, t[2 * s], t[2 * s + 1], 0, 0)
            ),
        ),
        out_shape=jax.ShapeDtypeStruct(shape, mine.dtype),
        input_output_aliases={} if whole is None else {3: 0},
        compiler_params=pltpu.CompilerParams(vmem_limit_bytes=8 * MIB),
        cost_estimate=pl.CostEstimate(
            flops=FILL_FLOPS, bytes_accessed=4 * n * nx * rows_v * width, transcendentals=0
        ),
    )(*operands)


def local(inputs, out_grads, proj_in, proj_out, store, valid, owner):
    yl, x, z, c, yh = (lax.axis_index(a) for a in ("yl", "x", "z", "c", "yh"))
    nx, nz, nc = SIZES["x"], SIZES["z"], SIZES["c"]
    examples = inputs.shape[0]
    rows_v, half = valid.shape
    rows_b = nx * rows_v
    rows_s = nc * examples

    def at(y):
        return (y % 2) * 2 + y // 2

    near = lax.ppermute(valid, ("yl", "yh"), [(at(i), at(j)) for i, j in ((0, 1), (1, 3), (2, 0), (3, 2))])
    cross = lax.ppermute(valid, ("yl", "yh"), [(at(1), at(2)), (at(2), at(1))])
    here = jnp.concatenate(
        [jnp.where(yl == yh, valid, near), jnp.where(yl == yh, near, cross)], axis=1
    )

    known = make_sketch(inputs, out_grads, proj_in, proj_out)
    known = jnp.concatenate([known, paired(known, "yl", 1)], axis=0)

    known, waited = lax.optimization_barrier((known, store))
    other = shifted(waited, "yh", 1)

    known = jnp.concatenate([known, paired(known, "x", 1)], axis=0)
    known, here = lax.optimization_barrier((known, here))

    pieces = [here] + [shifted(here, "x", k) for k in range(1, nx)]
    block = jnp.zeros((nx, rows_v, 2 * half), valid.dtype)
    for k, piece in enumerate(pieces):
        block = lax.dynamic_update_slice(block, piece[None], ((x - k) % nx, 0, 0))
    block = block.reshape(rows_b, 2 * half)

    whole = [None]

    def fill_all(mine, twin, steps):
        froms = [((z + step) % nz, c) for step in steps] + [((z + step) % nz, 1 - c) for step in steps]
        table = jnp.stack([part for pair in froms for part in pair]).astype(jnp.int32)
        shape = (nx, nz, nc, rows_v, 2 * half)
        whole[0] = filled(whole[0], shape, mine, twin, table)

    def both_ways(ahead, back):
        ahead, back = lax.optimization_barrier((ahead, back))
        return lax.optimization_barrier((shifted(ahead, "z", 1), shifted(back, "z", -1)))

    twin = shifted(block, "c", 1)
    up, down = both_ways(block, block)
    fill_all(block, twin, (0,))

    known = jnp.concatenate([known, paired(known, "x", 2)], axis=0)

    def dp_index(yl_, x_, z_, c_):
        return ((yl_ * nx + x_) * nz + z_) * nc + c_

    each = jnp.arange(examples, dtype=jnp.int32)
    from_x = x ^ jnp.arange(nx, dtype=jnp.int32)
    from_yl = yl ^ jnp.arange(2, dtype=jnp.int32)
    example = dp_index(from_yl[None, :, None], from_x[:, None, None], z, c) * examples + each
    number = jnp.arange(owner.shape[0], dtype=jnp.int32)
    slot_of = jnp.sum(jnp.where(example.reshape(-1, 1) == number, owner, 0), axis=1)
    to_z = (z + jnp.arange(nz, dtype=jnp.int32)) % nz
    to = dp_index(yl, x, to_z[:, None], jnp.arange(nc, dtype=jnp.int32))
    slot = (to[:, :, None] * examples + each).reshape(-1)
    picker = (slot[:, None] == slot_of[None, :]).astype(jnp.bfloat16)
    shares = jnp.dot(picker, known, preferred_element_type=jnp.float32).astype(jnp.bfloat16)
    shares = jnp.pad(shares, ((0, 0), (0, half)))

    def share(offset):
        first = (offset % nz) * rows_s
        return shares[first : first + rows_s]

    for k in (1, 2, 3):
        mine = jnp.concatenate([up[:rows_b], down[:rows_b]], axis=0)
        twin = shifted(mine, "c", 1)
        s_up, s_down = share(4 - k), share(k - 4)
        if k > 1:
            s_up, s_down = s_up + up[rows_b:], s_down + down[rows_b:]
        if k < 3:
            ahead, back = up[:rows_b], down[:rows_b]
        else:
            ahead, back = up[: rows_b // 2], down[rows_b // 2 : rows_b]
        up, down = both_ways(
            jnp.concatenate([ahead, s_up], axis=0), jnp.concatenate([back, s_down], axis=0)
        )
        fill_all(mine, twin, (-k, k))
        if k == 1:
            s_far = shifted(share(4), "z", 4)
    cut = rows_b // 2
    far = jnp.concatenate([up[:cut], down[:cut]], axis=0)
    fresh = (up[cut:] + down[cut:]) + (s_far + share(0))
    fresh = fresh.reshape(nc, examples, 2 * half)
    leave = jnp.where(c == 0, fresh[1], fresh[0])
    got = shifted(jnp.concatenate([far, leave], axis=0), "c", 1)
    fill_all(far, got[:rows_b], (4,))
    fresh = jnp.where(c == 0, fresh[0], fresh[1]) + got[rows_b:]

    fresh = jnp.pad(fresh[:, :half], ((0, 16 - examples), (0, 0)))
    fresh_other = shifted(fresh, "yh", 1)
    valid_all = whole[0].reshape(nx * nz * nc * rows_v, 2 * half)
    own = own_scores(store, valid_all, fresh, examples)
    other, own = lax.optimization_barrier((other, own))
    other = lax.dynamic_update_slice(other, fresh_other[:examples], (0, 0))
    return last_scores(other, valid_all, own, (2 * half) ** (-0.5))


def solution(mesh):
    fine = Mesh(mesh.devices.reshape(2, 4, 8, 2, 2), ("yl", "x", "z", "c", "yh"))
    return jax.shard_map(
        local,
        mesh=fine,
        in_specs=(
            P(DP, None, None),
            P(DP, None, None),
            P(),
            P(None, "yh"),
            P(DP, "yh"),
            P(DP, "yh"),
            P(),
        ),
        out_specs=P(DP, "yh"),
        check_vma=False,
    )
```

```python
import functools

import jax
import jax.numpy as jnp
from jax import lax
from jax.experimental import pallas as pl
from jax.experimental.pallas import tpu as pltpu
from jax.sharding import Mesh, PartitionSpec as P

DP = ("yl", "x", "z", "c")
SIZES = {"yl": 2, "x": 4, "z": 8, "c": 2, "yh": 2}
MIB = 1024 * 1024
BLOCK = 256
WIDE = 512
FILL_FLOPS = 20_000_000_000


def shifted(array, axis, by):
    size = SIZES[axis]
    return lax.ppermute(array, axis, [(i, (i + by) % size) for i in range(size)])


def paired(array, axis, bit):
    size = SIZES[axis]
    return lax.ppermute(array, axis, [(i, i ^ bit) for i in range(size)])


def dot_t(left, right):
    return lax.dot_general(
        left, right, (((1,), (1,)), ((), ())), preferred_element_type=jnp.float32
    )


def make_sketch(inputs, out_grads, proj_in, proj_out):
    examples, length, width_in = inputs.shape
    width_out = out_grads.shape[2]
    lin = jnp.dot(
        inputs.reshape(examples * length, width_in), proj_in, preferred_element_type=jnp.float32
    ).astype(jnp.bfloat16)
    lout = jnp.dot(
        out_grads.reshape(examples * length, width_out),
        proj_out,
        preferred_element_type=jnp.float32,
    ).astype(jnp.bfloat16)
    lin = lin.reshape(examples, length, -1)
    lout = lout.reshape(examples, length, -1)
    sketch = jnp.einsum("nso,nsi->noi", lout, lin, preferred_element_type=jnp.float32) * length ** (
        -0.5
    )
    return sketch.reshape(examples, -1).astype(jnp.bfloat16)


def own_kernel(examples, store_ref, valid_ref, fresh_ref, out_ref):
    out_ref[...] = dot_t(store_ref[...], valid_ref[...])
    n = fresh_ref.shape[0]
    value = dot_t(fresh_ref[...], valid_ref[...])
    row = lax.broadcasted_iota(jnp.int32, value.shape, 0)
    out_ref[:n] = jnp.where(row < examples, value, out_ref[:n])


def own_scores(store, valid, fresh, examples):
    rows, half = store.shape
    columns = valid.shape[0]
    whole = lambda array: pl.BlockSpec(array.shape, lambda i: (0, 0), pipeline_mode=pl.Buffered(1))
    return pl.pallas_call(
        functools.partial(own_kernel, examples),
        grid=(columns // BLOCK,),
        in_specs=[
            whole(store),
            pl.BlockSpec((BLOCK, half), lambda i: (i, 0)),
            whole(fresh),
        ],
        out_specs=pl.BlockSpec((rows, BLOCK), lambda i: (0, i)),
        out_shape=jax.ShapeDtypeStruct((rows, columns), jnp.float32),
        compiler_params=pltpu.CompilerParams(vmem_limit_bytes=16 * MIB),
        cost_estimate=pl.CostEstimate(flops=0, bytes_accessed=0, transcendentals=0),
    )(store, valid, fresh)


def last_kernel(factor, other_ref, valid_ref, own_ref, out_ref):
    total = own_ref[...] + dot_t(other_ref[...], valid_ref[...])
    out_ref[...] = (total * factor).astype(out_ref.dtype)


def last_scores(other, valid, own, factor):
    rows, half = other.shape
    columns = valid.shape[0]
    return pl.pallas_call(
        functools.partial(last_kernel, factor),
        grid=(columns // WIDE,),
        in_specs=[
            pl.BlockSpec((rows, half), lambda i: (0, 0), pipeline_mode=pl.Buffered(1)),
            pl.BlockSpec((WIDE, half), lambda i: (i, 1)),
            pl.BlockSpec((rows, WIDE), lambda i: (0, i)),
        ],
        out_specs=pl.BlockSpec((rows, WIDE), lambda i: (0, i)),
        out_shape=jax.ShapeDtypeStruct((rows, columns), jnp.bfloat16),
        compiler_params=pltpu.CompilerParams(vmem_limit_bytes=24 * MIB),
        cost_estimate=pl.CostEstimate(flops=0, bytes_accessed=0, transcendentals=0),
    )(other, valid, own)


def fill_kernel(table_ref, mine_ref, twin_ref, *refs):
    out_ref = refs[-1]
    n = pl.num_programs(0) // 2

    @pl.when(pl.program_id(0) < n)
    def _():
        out_ref[:, 0, 0] = mine_ref[0]

    @pl.when(pl.program_id(0) >= n)
    def _():
        out_ref[:, 0, 0] = twin_ref[0]


def filled(whole, shape, mine, twin, table):
    nx, _, _, rows_v, width = shape
    n = mine.shape[0] // (nx * rows_v)
    operands = [table, mine.reshape(n, nx, rows_v, width), twin.reshape(n, nx, rows_v, width)]
    specs = [
        pl.BlockSpec((1, nx, rows_v, width), lambda s, t: (jnp.minimum(s, n - 1), 0, 0, 0)),
        pl.BlockSpec((1, nx, rows_v, width), lambda s, t: (jnp.maximum(s - n, 0), 0, 0, 0)),
    ]
    if whole is not None:
        operands.append(whole)
        specs.append(pl.BlockSpec(memory_space=pl.ANY))
    return pl.pallas_call(
        fill_kernel,
        grid_spec=pltpu.PrefetchScalarGridSpec(
            num_scalar_prefetch=1,
            grid=(2 * n,),
            in_specs=specs,
            out_specs=pl.BlockSpec(
                (nx, 1, 1, rows_v, width), lambda s, t: (0, t[2 * s], t[2 * s + 1], 0, 0)
            ),
        ),
        out_shape=jax.ShapeDtypeStruct(shape, mine.dtype),
        input_output_aliases={} if whole is None else {3: 0},
        compiler_params=pltpu.CompilerParams(vmem_limit_bytes=8 * MIB),
        cost_estimate=pl.CostEstimate(
            flops=FILL_FLOPS, bytes_accessed=4 * n * nx * rows_v * width, transcendentals=0
        ),
    )(*operands)


def local(inputs, out_grads, proj_in, proj_out, store, valid, owner):
    yl, x, z, c, yh = (lax.axis_index(a) for a in ("yl", "x", "z", "c", "yh"))
    nx, nz, nc = SIZES["x"], SIZES["z"], SIZES["c"]
    examples = inputs.shape[0]
    rows_v, half = valid.shape
    rows_b = nx * rows_v
    rows_s = nc * examples

    def at(y):
        return (y % 2) * 2 + y // 2

    near = lax.ppermute(valid, ("yl", "yh"), [(at(i), at(j)) for i, j in ((0, 1), (1, 3), (2, 0), (3, 2))])
    cross = lax.ppermute(valid, ("yl", "yh"), [(at(1), at(2)), (at(2), at(1))])
    here = jnp.concatenate(
        [jnp.where(yl == yh, valid, near), jnp.where(yl == yh, near, cross)], axis=1
    )

    known = make_sketch(inputs, out_grads, proj_in, proj_out)
    known = jnp.concatenate([known, paired(known, "yl", 1)], axis=0)

    known, waited = lax.optimization_barrier((known, store))
    other = shifted(waited, "yh", 1)

    known = jnp.concatenate([known, paired(known, "x", 1)], axis=0)
    known, here = lax.optimization_barrier((known, here))

    pieces = [here] + [shifted(here, "x", k) for k in range(1, nx)]
    block = jnp.zeros((nx, rows_v, 2 * half), valid.dtype)
    for k, piece in enumerate(pieces):
        block = lax.dynamic_update_slice(block, piece[None], ((x - k) % nx, 0, 0))
    block = block.reshape(rows_b, 2 * half)

    whole = [None]

    def fill_all(mine, twin, steps):
        froms = [((z + step) % nz, c) for step in steps] + [((z + step) % nz, 1 - c) for step in steps]
        table = jnp.stack([part for pair in froms for part in pair]).astype(jnp.int32)
        shape = (nx, nz, nc, rows_v, 2 * half)
        whole[0] = filled(whole[0], shape, mine, twin, table)

    def both_ways(ahead, back):
        ahead, back = lax.optimization_barrier((ahead, back))
        return lax.optimization_barrier((shifted(ahead, "z", 1), shifted(back, "z", -1)))

    twin = shifted(block, "c", 1)
    up, down = both_ways(block, block)
    fill_all(block, twin, (0,))

    known = jnp.concatenate([known, paired(known, "x", 2)], axis=0)

    def dp_index(yl_, x_, z_, c_):
        return ((yl_ * nx + x_) * nz + z_) * nc + c_

    each = jnp.arange(examples, dtype=jnp.int32)
    from_x = x ^ jnp.arange(nx, dtype=jnp.int32)
    from_yl = yl ^ jnp.arange(2, dtype=jnp.int32)
    example = dp_index(from_yl[None, :, None], from_x[:, None, None], z, c) * examples + each
    number = jnp.arange(owner.shape[0], dtype=jnp.int32)
    slot_of = jnp.sum(jnp.where(example.reshape(-1, 1) == number, owner, 0), axis=1)
    to_z = (z + jnp.arange(nz, dtype=jnp.int32)) % nz
    to = dp_index(yl, x, to_z[:, None], jnp.arange(nc, dtype=jnp.int32))
    slot = (to[:, :, None] * examples + each).reshape(-1)
    picker = (slot[:, None] == slot_of[None, :]).astype(jnp.bfloat16)
    shares = jnp.dot(picker, known, preferred_element_type=jnp.float32).astype(jnp.bfloat16)
    shares = jnp.pad(shares, ((0, 0), (0, half)))

    def share(offset):
        first = (offset % nz) * rows_s
        return shares[first : first + rows_s]

    for k in (1, 2, 3):
        mine = jnp.concatenate([up[:rows_b], down[:rows_b]], axis=0)
        twin = shifted(mine, "c", 1)
        s_up, s_down = share(4 - k), share(k - 4)
        if k > 1:
            s_up, s_down = s_up + up[rows_b:], s_down + down[rows_b:]
        if k < 3:
            ahead, back = up[:rows_b], down[:rows_b]
        else:
            ahead, back = up[: rows_b // 2], down[rows_b // 2 : rows_b]
        up, down = both_ways(
            jnp.concatenate([ahead, s_up], axis=0), jnp.concatenate([back, s_down], axis=0)
        )
        fill_all(mine, twin, (-k, k))
        if k == 1:
            s_far = shifted(share(4), "z", 4)
    cut = rows_b // 2
    far = jnp.concatenate([up[:cut], down[:cut]], axis=0)
    fresh = (up[cut:] + down[cut:]) + (s_far + share(0))
    fresh = fresh.reshape(nc, examples, 2 * half)
    leave = jnp.where(c == 0, fresh[1], fresh[0])
    got = shifted(jnp.concatenate([far, leave], axis=0), "c", 1)
    fill_all(far, got[:rows_b], (4,))
    fresh = jnp.where(c == 0, fresh[0], fresh[1]) + got[rows_b:]

    fresh = jnp.pad(fresh[:, :half], ((0, 16 - examples), (0, 0)))
    fresh_other = shifted(fresh, "yh", 1)
    valid_all = whole[0].reshape(nx * nz * nc * rows_v, 2 * half)
    own = own_scores(store, valid_all, fresh, examples)
    other, own = lax.optimization_barrier((other, own))
    other = lax.dynamic_update_slice(other, fresh_other[:examples], (0, 0))
    return last_scores(other, valid_all, own, (2 * half) ** (-0.5))


def solution(mesh):
    fine = Mesh(mesh.devices.reshape(2, 4, 8, 2, 2), ("yl", "x", "z", "c", "yh"))
    return jax.shard_map(
        local,
        mesh=fine,
        in_specs=(
            P(DP, None, None),
            P(DP, None, None),
            P(),
            P(None, "yh"),
            P(DP, "yh"),
            P(DP, "yh"),
            P(),
        ),
        out_specs=P(DP, "yh"),
        check_vma=False,
    )
```
